32 devices in a mesh: groups: 2 (over y), dp: 4 (over z), tensor: 4 (over x, core).
Axes of the slice: x: 2, y: 2, z: 4, core: 2. Of those that a mesh axis runs over, the one named last changes fastest.
Arguments:
- queries: bfloat16 [2048, 5120], P(('groups', 'dp'), 'tensor'), parts along dimension 0, may hold values from -150 to 150
- suffix_keys: bfloat16 [2048, 1024], P(('groups', 'dp'), 'tensor'), parts along dimension 0, may hold values from -10 to 10
- suffix_values: bfloat16 [2048, 1024], P(('groups', 'dp'), 'tensor'), parts along dimension 0, may hold values from -6 to 6
- prefix_keys: bfloat16 [512, 1024], P(('groups', 'dp'), 'tensor'), parts along dimension 0, may hold values from -6 to 6
- prefix_values: bfloat16 [512, 1024], P(('groups', 'dp'), 'tensor'), parts along dimension 0, may hold values from -6 to 6
- grad_out: bfloat16 [2048, 5120], P(('groups', 'dp'), 'tensor'), parts along dimension 0, may hold values from -6 to 6
- parents: int32 [8], P('groups'), parts along dimension 0, may hold values from -1 to 2, as said below
- leaves: int32 [16], P(('groups', 'dp')), parts along dimension 0, may hold values from 0 to 3
- node_len: int32 [8], P('groups'), parts along dimension 0, may hold values from 1 to 64
Outputs:
- grad_queries: bfloat16 [2048, 5120], P(('groups', 'dp'), 'tensor'), parts along dimension 0
- grad_suffix_keys: bfloat16 [2048, 1024], P(('groups', 'dp'), 'tensor'), parts along dimension 0
- grad_suffix_values: bfloat16 [2048, 1024], P(('groups', 'dp'), 'tensor'), parts along dimension 0
- grad_prefix_keys: bfloat16 [512, 1024], P(('groups', 'dp'), 'tensor'), parts along dimension 0
- grad_prefix_values: bfloat16 [512, 1024], P(('groups', 'dp'), 'tensor'), parts along dimension 0
The draws below stay inside these ranges and needn't reach their ends.
There are 2 independent parts, one for each index of `groups`. The reference program is written for one: setup_inputs(seed, part) draws one part's arguments, and reference() takes and returns one part's arrays. A program takes and returns all parts, laid end to end along the dimension named above; each array names one. Nothing has to cross between parts.
Inputs may be any that keep to these rules, and one draw needn't show every extreme that they name: parents[n] < n; a -1 marks the root of a tree.
All inputs are finite; a program needn't handle non-finite values.
Results may differ from the reference program's by a relative error of at most 0.0051.
Values may be sent and summed in bfloat16 or wider, within the bound.
A program may use at most 64 MiB of HBM per device.

```python
import jax
import jax.numpy as jnp
from jax import lax

QH = 40
KVH = 8
HD = 128
BLK = 64
SUF = 128
NODES = 4
BRANCHES = 8


def shared_keys(key):
    base_keys = jax.random.normal(key, (BRANCHES * SUF, KVH * HD), jnp.float32)
    row_ids = jnp.arange(BRANCHES * SUF)
    shifted = jnp.roll(base_keys, -1, axis=0)
    return jnp.where((row_ids % 32 == 4)[:, None], 0.99 * shifted, base_keys)


def draw_suffix_keys(key, part):
    base_keys = shared_keys(key)
    return base_keys.astype(jnp.bfloat16)


def draw_queries(key, part):
    key = jax.random.fold_in(key, 22)
    first_key = jax.random.fold_in(key, 0)
    row_count = BRANCHES * SUF
    values = jax.random.normal(first_key, (row_count, QH * HD), jnp.float32)
    return values.astype(jnp.bfloat16)


def draw_parents(key, part):
    key = jax.random.fold_in(key, 11)
    first_key, second_key = jax.random.split(key)
    node_ids = jnp.arange(NODES, dtype=jnp.int32)
    backward = jax.random.randint(first_key, (NODES,), 0, 4, jnp.int32)
    rooted = jax.random.randint(second_key, (NODES,), 0, 8, jnp.int32) == 0
    parent_ids = node_ids - 1 - backward
    parent_ids = jnp.where((parent_ids < 0) | rooted, -1, parent_ids)
    return jnp.where(node_ids == NODES - 1, NODES - 2, parent_ids).astype(jnp.int32)


def draw_node_len(key, part):
    key = jax.random.fold_in(key, 12)
    first_key, second_key = jax.random.split(key)
    lengths = jax.random.randint(first_key, (NODES,), 1, BLK + 1, jnp.int32)
    chosen = jax.random.randint(second_key, (), 0, NODES, jnp.int32)
    return jnp.where(jnp.arange(NODES, dtype=jnp.int32) == chosen, BLK, lengths).astype(jnp.int32)


def with_ends(values, own_key, smallest, high):
    shape = values.shape
    place = [jax.random.randint(jax.random.fold_in(own_key, axis), (), 0, shape[axis]) for axis in range(len(shape))]
    values = values.at[tuple(place)].set(smallest)
    longest = shape.index(max(shape))
    place[longest] = (place[longest] + 1) % shape[longest]
    return values.at[tuple(place)].set(high)


def block_scale(stream_key, dims, pieces, low, high):
    level = 1.0
    for axis_at, parts in pieces:
        steps = jax.random.uniform(jax.random.fold_in(jax.random.fold_in(stream_key, 6), axis_at), (parts,), jnp.float32, low / len(pieces), high / len(pieces))
        level = level * jnp.repeat(jnp.exp(steps), dims[axis_at] // parts).reshape((-1,) + (1,) * (len(dims) - 1 - axis_at))
    return level


def centred(rng, dims, width, limit, shards=(), kind=jnp.bfloat16):
    gain = block_scale(rng, dims, shards, -0.22, 0.18) if shards else 1.0
    values = jax.random.normal(rng, dims, jnp.float32) * width * gain
    return jnp.minimum(jnp.maximum(values, -limit), limit).astype(kind)


def setup_inputs(seed: int = 0, part: int = 0) -> dict:
    seeds = jax.random.split(jax.random.key(seed), 10)
    part_keys = jax.random.split(jax.random.fold_in(seeds[9], part), 10)
    queries = draw_queries(jax.random.fold_in(jax.random.fold_in(seeds[9], part), 71), part)
    suffix_keys = draw_suffix_keys(jax.random.fold_in(jax.random.fold_in(seeds[9], part), 71), part)
    suffix_values = centred(part_keys[2], (BRANCHES * SUF, KVH * HD), 1.0, 6.0, ((0, 4), (1, 4)))
    prefix_keys = centred(part_keys[3], (NODES * BLK, KVH * HD), 1.0, 6.0, ((0, 4), (1, 4)))
    prefix_values = centred(part_keys[4], (NODES * BLK, KVH * HD), 1.0, 6.0, ((0, 4), (1, 4)))
    grad_out = centred(part_keys[5], (BRANCHES * SUF, QH * HD), 1.0, 6.0, ((0, 4), (1, 4)))
    parents = draw_parents(jax.random.fold_in(jax.random.fold_in(seeds[9], part), 71), part)
    leaves = with_ends(jax.random.randint(part_keys[7], (BRANCHES,), 0, NODES), jax.random.fold_in(part_keys[7], 1), 0, NODES - 1).astype(jnp.int32)
    node_len = draw_node_len(jax.random.fold_in(jax.random.fold_in(seeds[9], part), 71), part)
    return {"queries": queries, "suffix_keys": suffix_keys, "suffix_values": suffix_values, "prefix_keys": prefix_keys, "prefix_values": prefix_values, "grad_out": grad_out, "parents": parents, "leaves": leaves, "node_len": node_len}


def ancestry(leaves, parents):
    node_ids = jnp.arange(parents.shape[0], dtype=jnp.int32)

    def climb_step(position, running):
        on_path, current = running
        node_hot = current[:, None] == node_ids[None, :]
        upward = jnp.sum(jnp.where(node_hot, parents[None, :], 0), axis=1)
        current = jnp.where(jnp.any(node_hot, axis=1), upward, -1).astype(jnp.int32)
        return on_path | node_hot, current

    start_path = jnp.zeros((leaves.shape[0], parents.shape[0]), dtype=jnp.bool_)
    on_path, current = lax.fori_loop(0, parents.shape[0], climb_step, (start_path, leaves.astype(jnp.int32)))
    return on_path


def reference(queries, suffix_keys, suffix_values, prefix_keys, prefix_values, grad_out, parents, leaves, node_len):
    on_path = ancestry(leaves, parents)
    slot_count = NODES * BLK
    slot_ids = jnp.arange(slot_count, dtype=jnp.int32)
    node_of = slot_ids // BLK
    slot_live = (slot_ids % BLK) < node_len[node_of]
    group_size = QH // KVH
    score_scale = HD ** -0.5
    kv_width = KVH * HD
    token_ids = jnp.arange(SUF, dtype=jnp.int32)
    causal = token_ids[None, :] <= token_ids[:, None]

    def branch_step(summed, branch_id):
        first_row = (branch_id * SUF).astype(jnp.int32)
        query_rows = lax.dynamic_slice_in_dim(queries, first_row, SUF, 0).astype(jnp.float32).reshape(SUF, KVH, group_size, HD)
        grad_rows = lax.dynamic_slice_in_dim(grad_out, first_row, SUF, 0).astype(jnp.float32).reshape(SUF, KVH, group_size, HD)
        key_rows = jnp.concatenate([prefix_keys, lax.dynamic_slice_in_dim(suffix_keys, first_row, SUF, 0)], 0)
        value_rows = jnp.concatenate([prefix_values, lax.dynamic_slice_in_dim(suffix_values, first_row, SUF, 0)], 0)
        key_rows = key_rows.astype(jnp.float32).reshape(-1, KVH, HD)
        value_rows = value_rows.astype(jnp.float32).reshape(-1, KVH, HD)
        prefix_ok = on_path[branch_id][node_of] & slot_live
        allowed = jnp.concatenate([jnp.broadcast_to(prefix_ok[None, :], (SUF, slot_count)), causal], 1)
        scores = jnp.einsum('skgd,nkd->kgsn', query_rows, key_rows) * score_scale
        grad_p = jnp.einsum('skgd,nkd->kgsn', grad_rows, value_rows)
        new_max = jnp.max(jnp.where(allowed, scores, -1e30), axis=-1, keepdims=True)
        raw_weights = jnp.where(allowed, jnp.exp(scores - new_max), 0.0)
        log_total = new_max + jnp.log(jnp.sum(raw_weights, axis=-1, keepdims=True))
        probs = jnp.where(allowed, jnp.exp(scores - log_total), 0.0)
        row_delta = jnp.sum(probs * grad_p, axis=-1, keepdims=True)
        grad_s = probs * (grad_p - row_delta)
        probs_half = lax.optimization_barrier(probs.astype(jnp.bfloat16)).astype(jnp.float32)
        grad_s_half = lax.optimization_barrier(grad_s.astype(jnp.bfloat16)).astype(jnp.float32)
        grad_q = score_scale * jnp.einsum('kgsn,nkd->skgd', grad_s_half, key_rows)
        grad_k = score_scale * jnp.einsum('kgsn,skgd->nkd', grad_s_half, query_rows)
        grad_v = jnp.einsum('kgsn,skgd->nkd', probs_half, grad_rows)
        grad_k = grad_k.reshape(-1, kv_width)
        grad_v = grad_v.reshape(-1, kv_width)
        summed = summed + jnp.concatenate([grad_k[:slot_count], grad_v[:slot_count]], 1)
        return summed, (grad_q.reshape(SUF, QH * HD).astype(jnp.bfloat16), grad_k[slot_count:].astype(jnp.bfloat16), grad_v[slot_count:].astype(jnp.bfloat16))

    summed, outputs = lax.scan(branch_step, jnp.zeros((slot_count, 2 * kv_width), jnp.float32), jnp.arange(BRANCHES, dtype=jnp.int32))
    grad_q_all, grad_k_all, grad_v_all = outputs
    return (grad_q_all.reshape(BRANCHES * SUF, QH * HD), grad_k_all.reshape(BRANCHES * SUF, kv_width), grad_v_all.reshape(BRANCHES * SUF, kv_width), summed[:, :kv_width].astype(jnp.bfloat16), summed[:, kv_width:].astype(jnp.bfloat16))
```

```python
import functools
import math

import jax
import jax.numpy as jnp
from jax import lax
from jax.experimental import pallas as pl
from jax.experimental.pallas import tpu as pltpu
from jax.sharding import PartitionSpec as P

HD = 128
BLK = 64
SUF = 128
SCALE = HD ** -0.5
EXP_SCALE = SCALE * math.log2(math.e)
LOW = -1e30
MESH = pl.DeviceIdType.MESH


def dot_nt(left, right):
    return lax.dot_general(
        left, right, (((1,), (1,)), ((), ())), preferred_element_type=jnp.float32
    )


def dot_nn(left, right):
    return jnp.dot(left, right, preferred_element_type=jnp.float32)


def over(count, step, start):
    if count == 1:
        return step(0, start)
    return lax.fori_loop(0, count, step, start)


def kernel(
    n,
    q_hbm, ks_hbm, vs_hbm, kp_hbm, vp_hbm, g_hbm, parents_ref, leaves_ref, len_ref,
    gq_ref, gks_ref, gvs_ref, gkp_ref, gvp_ref,
    q, g, ks, vs, kp, vp, w_s, gp_s, p_half, ds_half, bias, stats, own, sbuf, rbuf,
    in_sem, k_send, k_recv, v_send, v_recv, r_send, r_recv,
):
    rows, width = q.shape
    heads = width // HD
    kv = ks.shape[1] // HD
    group = heads // kv
    nb = rows // SUF
    local = kp_hbm.shape[0]
    slots = n * local
    chunk = min(slots, 256)
    chunks = slots // chunk
    me = lax.axis_index("dp")
    peers = [lax.rem(me + j, n) for j in range(1, n)]

    barrier = pltpu.get_barrier_semaphore()
    for peer in peers:
        pl.semaphore_signal(barrier, inc=1, device_id={"dp": peer}, device_id_type=MESH)

    part = group * HD
    loads = [
        pltpu.make_async_copy(ks_hbm, ks, in_sem.at[0]),
        pltpu.make_async_copy(vs_hbm, vs, in_sem.at[1]),
    ]
    for m in range(kv):
        cols = pl.ds(m * part, part)
        loads.append(pltpu.make_async_copy(q_hbm.at[:, cols], q.at[:, cols], in_sem.at[4 + 2 * m]))
        loads.append(pltpu.make_async_copy(g_hbm.at[:, cols], g.at[:, cols], in_sem.at[5 + 2 * m]))
    mine = pl.ds(pl.multiple_of(me * local, local), local)
    own_copies = [
        pltpu.make_async_copy(kp_hbm, kp.at[mine], in_sem.at[2]),
        pltpu.make_async_copy(vp_hbm, vp.at[mine], in_sem.at[3]),
    ]
    for copy in loads + own_copies:
        copy.start()

    pl.semaphore_wait(barrier, n - 1)
    gathers = []
    for src, dst, send, recv in ((kp_hbm, kp, k_send, k_recv), (vp_hbm, vp, v_send, v_recv)):
        for j, peer in enumerate(peers):
            copy = pltpu.make_async_remote_copy(
                src_ref=src, dst_ref=dst.at[mine], send_sem=send.at[j], recv_sem=recv.at[j],
                device_id={"dp": peer}, device_id_type=MESH,
            )
            copy.start()
            gathers.append(copy)

    nodes = len_ref.shape[0]
    place = lax.broadcasted_iota(jnp.int32, (BLK, SUF), 0)
    for b in range(nb):
        current = leaves_ref[b]
        for node in reversed(range(nodes)):
            hit = current == node
            live = jnp.where(hit, len_ref[node], 0)
            current = jnp.where(hit, parents_ref[node], current)
            bias[node * BLK:(node + 1) * BLK, b * SUF:(b + 1) * SUF] = jnp.where(
                place < live, 0.0, LOW
            )

    causal = lax.broadcasted_iota(jnp.int32, (SUF, SUF), 0) <= lax.broadcasted_iota(
        jnp.int32, (SUF, SUF), 1
    )
    hcol = lambda h: slice(h * HD, (h + 1) * HD)
    brow = lambda b: slice(b * SUF, (b + 1) * SUF)

    loads[0].wait()
    loads[1].wait()
    for h in range(heads):
        m = h // group
        if h % group == 0:
            loads[2 + 2 * m].wait()
            loads[3 + 2 * m].wait()
        for b in range(nb):
            s = dot_nt(ks[brow(b), hcol(m)], q[brow(b), hcol(h)])
            s = jnp.where(causal, s, LOW)
            gp = dot_nt(vs[brow(b), hcol(m)], g[brow(b), hcol(h)])
            top = jnp.max(s, axis=0, keepdims=True)
            w = jnp.exp2((s - top) * EXP_SCALE)
            w_s[h, :, brow(b)] = w
            gp_s[h, :, brow(b)] = gp
            stats[h, 0:1, brow(b)] = top
            stats[h, 1:2, brow(b)] = jnp.sum(w, axis=0, keepdims=True)
            stats[h, 2:3, brow(b)] = jnp.sum(w * gp, axis=0, keepdims=True)

    for copy in own_copies:
        copy.wait()
    for copy in gathers:
        copy.wait_recv()

    sends = []
    for m in range(kv):
        for i in range(group):
            h = m * group + i

            def at(c):
                if chunks == 1:
                    return slice(0, chunk)
                return pl.ds(pl.multiple_of(c * chunk, chunk), chunk)

            def scores(c):
                return dot_nt(kp[at(c), hcol(m)], q[:, hcol(h)]) + bias[at(c), :]

            def grads(c):
                return dot_nt(vp[at(c), hcol(m)], g[:, hcol(h)])

            if chunks == 1:
                only_s, only_g = scores(0), grads(0)
                scores, grads = (lambda c: only_s), (lambda c: only_g)
            top_s = stats[h, 0:1, :]
            top = over(
                chunks,
                lambda c, t: jnp.maximum(t, jnp.max(scores(c), axis=0, keepdims=True)),
                top_s,
            )
            shrink = jnp.exp2((top_s - top) * EXP_SCALE)
            weights = lambda c: jnp.exp2((scores(c) - top) * EXP_SCALE)
            if chunks == 1:
                only_w = weights(0)
                weights = lambda c: only_w

            def add_up(c, sums):
                w = weights(c)
                return (
                    sums[0] + jnp.sum(w, axis=0, keepdims=True),
                    sums[1] + jnp.sum(w * grads(c), axis=0, keepdims=True),
                )

            total, dotted = over(
                chunks, add_up, (stats[h, 1:2, :] * shrink, stats[h, 2:3, :] * shrink)
            )
            inverse = 1.0 / total
            delta = dotted * inverse
            stats[h, 3:4, :] = shrink * inverse
            stats[h, 4:5, :] = delta

            def finish(c, nothing):
                probs = weights(c) * inverse
                cols = slice(i * rows, (i + 1) * rows)
                p_half[m, at(c), cols] = probs.astype(jnp.bfloat16)
                ds_half[m, at(c), cols] = (probs * (grads(c) - delta)).astype(jnp.bfloat16)
                return nothing

            over(chunks, finish, 0)

        q_all = jnp.concatenate([q[:, hcol(m * group + i)] for i in range(group)], axis=0)
        g_all = jnp.concatenate([g[:, hcol(m * group + i)] for i in range(group)], axis=0)

        def reduce_node(d, nothing):
            at_d = pl.ds(pl.multiple_of(d * local, local), local)
            put(at_d, d, dot_nn(p_half[m, at_d, :], g_all), dot_nn(ds_half[m, at_d, :], q_all))
            return nothing

        def put(at_d, d, grad_v, grad_k):
            grad_k = grad_k * SCALE
            own[m, 0, at_d, :] = grad_k
            own[m, 1, at_d, :] = grad_v
            sbuf[m, d, 0] = grad_k.astype(jnp.bfloat16)
            sbuf[m, d, 1] = grad_v.astype(jnp.bfloat16)

        if chunks == 1:
            grad_v = dot_nn(p_half[m], g_all)
            grad_k = dot_nn(ds_half[m], q_all)
            for d in range(n):
                at_d = slice(d * local, (d + 1) * local)
                put(at_d, d, grad_v[at_d], grad_k[at_d])
        else:
            lax.fori_loop(0, n, reduce_node, 0)
        for j, peer in enumerate(peers):
            copy = pltpu.make_async_remote_copy(
                src_ref=sbuf.at[m, peer], dst_ref=rbuf.at[m, j],
                send_sem=r_send.at[m, j], recv_sem=r_recv.at[m, j],
                device_id={"dp": peer}, device_id_type=MESH,
            )
            copy.start()
            sends.append(copy)

    for m in range(kv):
        kp_t = kp[:, hcol(m)].T
        ks_t = [ks[brow(b), hcol(m)].T for b in range(nb)]
        p_parts = [[] for b in range(nb)]
        d_parts = [[] for b in range(nb)]
        for i in range(group):
            h = m * group + i
            probs = w_s[h] * stats[h, 3:4, :]
            ds = (probs * (gp_s[h] - stats[h, 4:5, :])).astype(jnp.bfloat16)
            probs = probs.astype(jnp.bfloat16)
            grad_q = dot_nn(kp_t, ds_half[m, :, i * rows:(i + 1) * rows])
            for b in range(nb):
                p_parts[b].append(probs[:, brow(b)])
                d_parts[b].append(ds[:, brow(b)])
                both = grad_q[:, brow(b)] + dot_nn(ks_t[b], ds[:, brow(b)])
                gq_ref[brow(b), hcol(h)] = (both * SCALE).T.astype(jnp.bfloat16)
        for b in range(nb):
            q_all = jnp.concatenate([q[brow(b), hcol(m * group + i)] for i in range(group)], axis=0)
            g_all = jnp.concatenate([g[brow(b), hcol(m * group + i)] for i in range(group)], axis=0)
            grad_v = dot_nn(jnp.concatenate(p_parts[b], axis=1), g_all)
            grad_k = dot_nn(jnp.concatenate(d_parts[b], axis=1), q_all) * SCALE
            gks_ref[brow(b), hcol(m)] = grad_k.astype(jnp.bfloat16)
            gvs_ref[brow(b), hcol(m)] = grad_v.astype(jnp.bfloat16)

    for copy in sends:
        copy.wait_recv()
    for m in range(kv):
        for which, out in ((0, gkp_ref), (1, gvp_ref)):
            summed = own[m, which, mine, :]
            for j in range(n - 1):
                summed = summed + rbuf[m, j, which].astype(jnp.float32)
            out[:, hcol(m)] = summed.astype(jnp.bfloat16)
    for copy in gathers + sends:
        copy.wait_send()


def body(n, queries, suffix_keys, suffix_values, prefix_keys, prefix_values, grad_out,
         parents, leaves, node_len):
    rows, width = queries.shape
    kv_width = suffix_keys.shape[1]
    heads, kv = width // HD, kv_width // HD
    group = heads // kv
    local = prefix_keys.shape[0]
    slots = n * local
    half, full = jnp.bfloat16, jnp.float32
    any_spec = pl.BlockSpec(memory_space=pl.ANY)
    smem = pl.BlockSpec(memory_space=pltpu.SMEM)
    vmem = pl.BlockSpec(memory_space=pltpu.VMEM)
    flops = 10 * rows * heads * HD * (slots + SUF)
    return pl.pallas_call(
        functools.partial(kernel, n),
        out_shape=(
            jax.ShapeDtypeStruct((rows, width), half),
            jax.ShapeDtypeStruct((rows, kv_width), half),
            jax.ShapeDtypeStruct((rows, kv_width), half),
            jax.ShapeDtypeStruct((local, kv_width), half),
            jax.ShapeDtypeStruct((local, kv_width), half),
        ),
        in_specs=[any_spec] * 6 + [smem] * 3,
        out_specs=(vmem,) * 5,
        scratch_shapes=[
            pltpu.VMEM((rows, width), half),
            pltpu.VMEM((rows, width), half),
            pltpu.VMEM((rows, kv_width), half),
            pltpu.VMEM((rows, kv_width), half),
            pltpu.VMEM((slots, kv_width), half),
            pltpu.VMEM((slots, kv_width), half),
            pltpu.VMEM((heads, SUF, rows), full),
            pltpu.VMEM((heads, SUF, rows), full),
            pltpu.VMEM((kv, slots, group * rows), half),
            pltpu.VMEM((kv, slots, group * rows), half),
            pltpu.VMEM((slots, rows), full),
            pltpu.VMEM((heads, 8, rows), full),
            pltpu.VMEM((kv, 2, slots, HD), full),
            pltpu.VMEM((kv, n, 2, local, HD), half),
            pltpu.VMEM((kv, n - 1, 2, local, HD), half),
            pltpu.SemaphoreType.DMA((4 + 2 * kv,)),
            pltpu.SemaphoreType.DMA((n - 1,)),
            pltpu.SemaphoreType.DMA((n - 1,)),
            pltpu.SemaphoreType.DMA((n - 1,)),
            pltpu.SemaphoreType.DMA((n - 1,)),
            pltpu.SemaphoreType.DMA((kv, n - 1)),
            pltpu.SemaphoreType.DMA((kv, n - 1)),
        ],
        compiler_params=pltpu.CompilerParams(
            collective_id=0, has_side_effects=True, vmem_limit_bytes=48 * 1024 * 1024
        ),
        cost_estimate=pl.CostEstimate(
            flops=flops, bytes_accessed=8 * rows * width, transcendentals=rows * heads * (slots + SUF)
        ),
    )(queries, suffix_keys, suffix_values, prefix_keys, prefix_values, grad_out,
      parents, leaves, node_len)


def solution(mesh):
    rows_cols = P(("groups", "dp"), "tensor")
    return jax.shard_map(
        functools.partial(body, mesh.shape["dp"]),
        mesh=mesh,
        in_specs=(rows_cols,) * 6 + (P("groups"), P(("groups", "dp")), P("groups")),
        out_specs=(rows_cols,) * 5,
        check_vma=False,
    )
```

```python
import functools
import math

import jax
import jax.numpy as jnp
from jax import lax
from jax.experimental import pallas as pl
from jax.experimental.pallas import tpu as pltpu
from jax.sharding import PartitionSpec as P

HD = 128
BLK = 64
SUF = 128
SCALE = HD ** -0.5
EXP_SCALE = SCALE * math.log2(math.e)
LOW = -1e30
LIMIT = 63 * 1024 * 1024
MESH = pl.DeviceIdType.MESH


def dot_nt(left, right):
    return lax.dot_general(
        left, right, (((1,), (1,)), ((), ())), preferred_element_type=jnp.float32
    )


def dot_nn(left, right):
    return jnp.dot(left, right, preferred_element_type=jnp.float32)


def over(count, step, start):
    if count == 1:
        return step(0, start)
    return lax.fori_loop(0, count, step, start)


def kernel(
    n,
    q_hbm, ks_hbm, vs_hbm, kp_hbm, vp_hbm, g_hbm, parents_hbm, leaves_hbm, len_hbm,
    gq_out, gks_out, gvs_out, gkp_out, gvp_out,
    q, g, ks, vs, kp, vp, w_s, gp_s, p_half, ds_half, bias, stats, own, sbuf, rbuf, xbuf,
    gq_ref, gks_ref, gvs_ref, gkp_ref, gvp_ref, parents_ref, leaves_ref, len_ref,
    in_sem, g_send, g_recv, r_send, r_recv, x_send, x_recv, out_sem,
):
    rows, width = q.shape
    heads = width // HD
    kv = ks.shape[1] // HD
    group = heads // kv
    nb = rows // SUF
    local = kp_hbm.shape[0]
    slots = n * local
    chunk = min(slots, 256)
    chunks = slots // chunk
    part = group * HD
    me = lax.axis_index("dp")
    relay = n == 4
    is_end = jnp.logical_or(me == 0, me == n - 1)
    is_mid = jnp.logical_not(is_end)
    across = n - 1 - me
    opposite = lax.rem(me + 2, n)
    beside = jnp.where(me == 0, 1, n - 2)
    hops = [2, 1, 3] if relay else list(range(1, n))
    peers = {j: lax.rem(me + j, n) for j in hops}
    hcol = lambda h: slice(h * HD, (h + 1) * HD)
    brow = lambda b: slice(b * SUF, (b + 1) * SUF)

    def when(condition, action):
        if condition is None:
            action()
        elif relay:
            pl.when(condition)(action)

    def direct(j):
        if not relay or j == 2:
            return None
        return me != (n - 1 if j == 1 else 0)

    def remote(src, dst, send, recv, device):
        return pltpu.make_async_remote_copy(
            src_ref=src, dst_ref=dst, send_sem=send, recv_sem=recv,
            device_id={"dp": device}, device_id_type=MESH,
        )

    barrier = pltpu.get_barrier_semaphore()
    for peer in peers.values():
        pl.semaphore_signal(barrier, inc=1, device_id={"dp": peer}, device_id_type=MESH)

    places = lambda d: pl.ds(pl.multiple_of(d * local, local), local)
    mine = places(me)
    small = [
        pltpu.make_async_copy(parents_hbm, parents_ref, in_sem.at[0]),
        pltpu.make_async_copy(leaves_hbm, leaves_ref, in_sem.at[1]),
        pltpu.make_async_copy(len_hbm, len_ref, in_sem.at[2]),
    ]
    loads = [
        pltpu.make_async_copy(ks_hbm, ks, in_sem.at[3]),
        pltpu.make_async_copy(vs_hbm, vs, in_sem.at[4]),
    ]
    for m in range(kv):
        cols = pl.ds(m * part, part)
        base = 5 + 4 * m
        loads.append(pltpu.make_async_copy(q_hbm.at[:, cols], q.at[:, cols], in_sem.at[base]))
        loads.append(pltpu.make_async_copy(g_hbm.at[:, cols], g.at[:, cols], in_sem.at[base + 1]))
    own_copies = []
    for m in range(kv):
        for w, (src, dst) in enumerate(((kp_hbm, kp), (vp_hbm, vp))):
            own_copies.append(
                pltpu.make_async_copy(src.at[:, hcol(m)], dst.at[m, mine], in_sem.at[7 + 4 * m + w])
            )
    for copy in small + loads + own_copies:
        copy.start()

    sent = []

    def start(condition, copy):
        when(condition, copy.start)
        sent.append((condition, copy))

    pl.semaphore_wait(barrier, len(hops))
    for m in range(kv):
        for w, (src, dst) in enumerate(((kp_hbm, kp), (vp_hbm, vp))):
            for j in hops:
                start(direct(j), remote(
                    src.at[:, hcol(m)], dst.at[m, mine], g_send.at[m, w, j], g_recv.at[m, w, me],
                    peers[j],
                ))

    def block_of(m, w, owner, device):
        held = (kp, vp)[w].at[m, places(owner)]
        return remote(held, held, g_send.at[m, w, 0], g_recv.at[m, w, owner], device)

    def pass_on(m):
        if relay:
            for w in range(2):
                block_of(m, w, opposite, across).wait_recv()
                start(is_mid, block_of(m, w, opposite, n - 1 - opposite))

    def wait_blocks(m):
        for w in range(2):
            for j in hops:
                if not relay or j != 2:
                    block_of(m, w, peers[j], peers[j]).wait_recv()

    def clear():
        rbuf[:, across] = jnp.zeros((kv,) + rbuf.shape[2:], rbuf.dtype)

    if relay:
        pl.when(is_end)(clear)
    for copy in small:
        copy.wait()
    nodes = len_ref.shape[0]
    place = lax.broadcasted_iota(jnp.int32, (BLK, SUF), 0)
    for b in range(nb):
        current = leaves_ref[b]
        for node in reversed(range(nodes)):
            hit = current == node
            live = jnp.where(hit, len_ref[node], 0)
            current = jnp.where(hit, parents_ref[node], current)
            bias[node * BLK:(node + 1) * BLK, b * SUF:(b + 1) * SUF] = jnp.where(
                place < live, 0.0, LOW
            )

    causal = lax.broadcasted_iota(jnp.int32, (SUF, SUF), 0) <= lax.broadcasted_iota(
        jnp.int32, (SUF, SUF), 1
    )

    loads[0].wait()
    loads[1].wait()
    for h in range(heads):
        m = h // group
        if h % group == 0:
            loads[2 + 2 * m].wait()
            loads[3 + 2 * m].wait()
        for b in range(nb):
            s = dot_nt(ks[brow(b), hcol(m)], q[brow(b), hcol(h)])
            s = jnp.where(causal, s, LOW)
            gp = dot_nt(vs[brow(b), hcol(m)], g[brow(b), hcol(h)])
            top = jnp.max(s, axis=0, keepdims=True)
            w = jnp.exp2((s - top) * EXP_SCALE)
            w_s[h, :, brow(b)] = w
            gp_s[h, :, brow(b)] = gp
            stats[h, 0:1, brow(b)] = top
            stats[h, 1:2, brow(b)] = jnp.sum(w, axis=0, keepdims=True)
            stats[h, 2:3, brow(b)] = jnp.sum(w * gp, axis=0, keepdims=True)

    def partial_to(m, j):
        return remote(
            sbuf.at[m, peers[j]], rbuf.at[m, me], r_send.at[m, j], r_recv.at[m, me], peers[j]
        )

    def partial_from(m, owner):
        return remote(sbuf.at[m, 0], rbuf.at[m, owner], r_send.at[m, 0], r_recv.at[m, owner], owner)

    def combine(m):
        def add():
            remote(sbuf.at[m, 0], xbuf.at[m], x_send.at[m], x_recv.at[m], beside).wait_recv()
            for w in range(2):
                joint = own[m, w, places(opposite), :] + xbuf[m, w].astype(jnp.float32)
                sbuf[m, opposite, w] = joint.astype(jnp.bfloat16)

        if relay:
            when(is_mid, add)
            start(is_mid, partial_to(m, 2))

    for copy in own_copies:
        copy.wait()
    pass_on(0)
    for m in range(kv):
        wait_blocks(m)
        for i in range(group):
            h = m * group + i
            if i == group // 2 and m + 1 < kv:
                pass_on(m + 1)

            def at(c):
                if chunks == 1:
                    return slice(0, chunk)
                return pl.ds(pl.multiple_of(c * chunk, chunk), chunk)

            def scores(c):
                return dot_nt(kp[m, at(c), :], q[:, hcol(h)]) + bias[at(c), :]

            def grads(c):
                return dot_nt(vp[m, at(c), :], g[:, hcol(h)])

            if chunks == 1:
                only_s, only_g = scores(0), grads(0)
                scores, grads = (lambda c: only_s), (lambda c: only_g)
            top_s = stats[h, 0:1, :]
            top = over(
                chunks,
                lambda c, t: jnp.maximum(t, jnp.max(scores(c), axis=0, keepdims=True)),
                top_s,
            )
            shrink = jnp.exp2((top_s - top) * EXP_SCALE)
            weights = lambda c: jnp.exp2((scores(c) - top) * EXP_SCALE)
            if chunks == 1:
                only_w = weights(0)
                weights = lambda c: only_w

            def add_up(c, sums):
                w = weights(c)
                return (
                    sums[0] + jnp.sum(w, axis=0, keepdims=True),
                    sums[1] + jnp.sum(w * grads(c), axis=0, keepdims=True),
                )

            total, dotted = over(
                chunks, add_up, (stats[h, 1:2, :] * shrink, stats[h, 2:3, :] * shrink)
            )
            inverse = 1.0 / total
            delta = dotted * inverse
            stats[h, 3:4, :] = shrink * inverse
            stats[h, 4:5, :] = delta

            def finish(c, nothing):
                probs = weights(c) * inverse
                cols = slice(i * rows, (i + 1) * rows)
                p_half[m, at(c), cols] = probs.astype(jnp.bfloat16)
                ds_half[m, at(c), cols] = (probs * (grads(c) - delta)).astype(jnp.bfloat16)
                return nothing

            over(chunks, finish, 0)

        q_all = jnp.concatenate([q[:, hcol(m * group + i)] for i in range(group)], axis=0)
        g_all = jnp.concatenate([g[:, hcol(m * group + i)] for i in range(group)], axis=0)

        def reduce_node(d, nothing):
            at_d = pl.ds(pl.multiple_of(d * local, local), local)
            put(at_d, d, dot_nn(p_half[m, at_d, :], g_all), dot_nn(ds_half[m, at_d, :], q_all))
            return nothing

        def put(at_d, d, grad_v, grad_k):
            grad_k = grad_k * SCALE
            own[m, 0, at_d, :] = grad_k
            own[m, 1, at_d, :] = grad_v
            sbuf[m, d, 0] = grad_k.astype(jnp.bfloat16)
            sbuf[m, d, 1] = grad_v.astype(jnp.bfloat16)

        if chunks == 1:
            grad_v = dot_nn(p_half[m], g_all)
            grad_k = dot_nn(ds_half[m], q_all)
            for d in range(n):
                at_d = slice(d * local, (d + 1) * local)
                put(at_d, d, grad_v[at_d], grad_k[at_d])
        else:
            lax.fori_loop(0, n, reduce_node, 0)
        if relay:
            start(is_end, remote(
                sbuf.at[m, across], xbuf.at[m], x_send.at[m], x_recv.at[m], beside
            ))
        for j in hops:
            condition = is_end if relay and j == 2 else direct(j)
            start(condition, partial_to(m, j))
        if m > 0:
            combine(m - 1)

    results = []
    for m in range(kv):
        kp_t = kp[m].T
        ks_t = [ks[brow(b), hcol(m)].T for b in range(nb)]
        p_parts = [[] for b in range(nb)]
        d_parts = [[] for b in range(nb)]
        for i in range(group):
            h = m * group + i
            probs = w_s[h] * stats[h, 3:4, :]
            ds = (probs * (gp_s[h] - stats[h, 4:5, :])).astype(jnp.bfloat16)
            probs = probs.astype(jnp.bfloat16)
            grad_q = dot_nn(kp_t, ds_half[m, :, i * rows:(i + 1) * rows])
            for b in range(nb):
                p_parts[b].append(probs[:, brow(b)])
                d_parts[b].append(ds[:, brow(b)])
                both = grad_q[:, brow(b)] + dot_nn(ks_t[b], ds[:, brow(b)])
                gq_ref[brow(b), hcol(h)] = (both * SCALE).T.astype(jnp.bfloat16)
        for b in range(nb):
            q_all = jnp.concatenate([q[brow(b), hcol(m * group + i)] for i in range(group)], axis=0)
            g_all = jnp.concatenate([g[brow(b), hcol(m * group + i)] for i in range(group)], axis=0)
            grad_v = dot_nn(jnp.concatenate(p_parts[b], axis=1), g_all)
            grad_k = dot_nn(jnp.concatenate(d_parts[b], axis=1), q_all) * SCALE
            gks_ref[brow(b), hcol(m)] = grad_k.astype(jnp.bfloat16)
            gvs_ref[brow(b), hcol(m)] = grad_v.astype(jnp.bfloat16)
        cols = pl.ds(m * part, part)
        results.append(
            pltpu.make_async_copy(gq_ref.at[:, cols], gq_out.at[:, cols], out_sem.at[4 + m])
        )
        results[-1].start()
        if m == kv - 1:
            results.append(pltpu.make_async_copy(gks_ref, gks_out, out_sem.at[2]))
            results.append(pltpu.make_async_copy(gvs_ref, gvs_out, out_sem.at[3]))
            results[-2].start()
            results[-1].start()

    combine(kv - 1)
    for m in range(kv):
        for j in hops:
            if not relay or j == 2:
                condition = None
            else:
                condition = direct(j)
            when(condition, partial_from(m, peers[j]).wait_recv)
        for w, out in ((0, gkp_ref), (1, gvp_ref)):
            summed = own[m, w, mine, :]
            for j in hops:
                summed = summed + rbuf[m, peers[j], w].astype(jnp.float32)
            out[:, hcol(m)] = summed.astype(jnp.bfloat16)
    last = [
        pltpu.make_async_copy(gkp_ref, gkp_out, out_sem.at[0]),
        pltpu.make_async_copy(gvp_ref, gvp_out, out_sem.at[1]),
    ]
    for copy in last:
        copy.start()
    for condition, copy in sent:
        when(condition, copy.wait_send)
    for copy in results + last:
        copy.wait()


def write_out(*refs):
    sources, outs, held, sems = refs[:5], refs[5:10], refs[10:15], refs[15]
    loads = [pltpu.make_async_copy(a, b, sems.at[0, i]) for i, (a, b) in enumerate(zip(sources, held))]
    stores = [pltpu.make_async_copy(a, b, sems.at[1, i]) for i, (a, b) in enumerate(zip(held, outs))]
    for copy in loads:
        copy.start()
    for load, store in zip(loads, stores):
        load.wait()
        store.start()
    for copy in stores:
        copy.wait()


def body(n, queries, suffix_keys, suffix_values, prefix_keys, prefix_values, grad_out,
         parents, leaves, node_len):
    rows, width = queries.shape
    kv_width = suffix_keys.shape[1]
    heads, kv = width // HD, kv_width // HD
    group = heads // kv
    local = prefix_keys.shape[0]
    slots = n * local
    half, full = jnp.bfloat16, jnp.float32
    hbm = pl.BlockSpec(memory_space=pl.ANY)
    flops = 10 * rows * heads * HD * (slots + SUF)
    results = pl.pallas_call(
        functools.partial(kernel, n),
        out_shape=(
            jax.ShapeDtypeStruct((rows, width), half),
            jax.ShapeDtypeStruct((rows, kv_width), half),
            jax.ShapeDtypeStruct((rows, kv_width), half),
            jax.ShapeDtypeStruct((local, kv_width), half),
            jax.ShapeDtypeStruct((local, kv_width), half),
        ),
        in_specs=[hbm] * 9,
        out_specs=(hbm,) * 5,
        scratch_shapes=[
            pltpu.VMEM((rows, width), half),
            pltpu.VMEM((rows, width), half),
            pltpu.VMEM((rows, kv_width), half),
            pltpu.VMEM((rows, kv_width), half),
            pltpu.VMEM((kv, slots, HD), half),
            pltpu.VMEM((kv, slots, HD), half),
            pltpu.VMEM((heads, SUF, rows), full),
            pltpu.VMEM((heads, SUF, rows), full),
            pltpu.VMEM((kv, slots, group * rows), half),
            pltpu.VMEM((kv, slots, group * rows), half),
            pltpu.VMEM((slots, rows), full),
            pltpu.VMEM((heads, 8, rows), full),
            pltpu.VMEM((kv, 2, slots, HD), full),
            pltpu.VMEM((kv, n, 2, local, HD), half),
            pltpu.VMEM((kv, n, 2, local, HD), half),
            pltpu.VMEM((kv, 2, local, HD), half),
            pltpu.VMEM((rows, width), half),
            pltpu.VMEM((rows, kv_width), half),
            pltpu.VMEM((rows, kv_width), half),
            pltpu.VMEM((local, kv_width), half),
            pltpu.VMEM((local, kv_width), half),
            pltpu.SMEM(parents.shape, jnp.int32),
            pltpu.SMEM(leaves.shape, jnp.int32),
            pltpu.SMEM(node_len.shape, jnp.int32),
            pltpu.SemaphoreType.DMA((5 + 4 * kv,)),
            pltpu.SemaphoreType.DMA((kv, 2, n)),
            pltpu.SemaphoreType.DMA((kv, 2, n)),
            pltpu.SemaphoreType.DMA((kv, n)),
            pltpu.SemaphoreType.DMA((kv, n)),
            pltpu.SemaphoreType.DMA((kv,)),
            pltpu.SemaphoreType.DMA((kv,)),
            pltpu.SemaphoreType.DMA((4 + kv,)),
        ],
        compiler_params=pltpu.CompilerParams(
            collective_id=0, has_side_effects=True, vmem_limit_bytes=LIMIT
        ),
        cost_estimate=pl.CostEstimate(
            flops=flops, bytes_accessed=8 * rows * width, transcendentals=rows * heads * (slots + SUF)
        ),
    )(queries, suffix_keys, suffix_values, prefix_keys, prefix_values, grad_out,
      parents, leaves, node_len)
    return pl.pallas_call(
        write_out,
        out_shape=tuple(jax.ShapeDtypeStruct(r.shape, r.dtype) for r in results),
        in_specs=[pl.BlockSpec(memory_space=pl.ANY)] * 5,
        out_specs=(hbm,) * 5,
        scratch_shapes=[pltpu.VMEM(r.shape, r.dtype) for r in results]
        + [pltpu.SemaphoreType.DMA((2, 5))],
        compiler_params=pltpu.CompilerParams(vmem_limit_bytes=LIMIT),
        cost_estimate=pl.CostEstimate(flops=0, bytes_accessed=4 * rows * width, transcendentals=0),
    )(*results)


def solution(mesh):
    rows_cols = P(("groups", "dp"), "tensor")
    return jax.shard_map(
        functools.partial(body, mesh.shape["dp"]),
        mesh=mesh,
        in_specs=(rows_cols,) * 6 + (P("groups"), P(("groups", "dp")), P("groups")),
        out_specs=(rows_cols,) * 5,
        check_vma=False,
    )
```

```python
import functools
import math

import jax
import jax.numpy as jnp
from jax import lax
from jax.experimental import pallas as pl
from jax.experimental.pallas import tpu as pltpu
from jax.sharding import PartitionSpec as P

HD = 128
BLK = 64
SUF = 128
SCALE = HD ** -0.5
EXP_SCALE = SCALE * math.log2(math.e)
LOW = -1e30
LIMIT = 63 * 1024 * 1024
MESH = pl.DeviceIdType.MESH


def dot_nt(left, right):
    return lax.dot_general(
        left, right, (((1,), (1,)), ((), ())), preferred_element_type=jnp.float32
    )


def dot_nn(left, right):
    return jnp.dot(left, right, preferred_element_type=jnp.float32)


def over(count, step, start):
    if count == 1:
        return step(0, start)
    return lax.fori_loop(0, count, step, start)


def kernel(
    n,
    q_hbm, ks_hbm, vs_hbm, kp_hbm, vp_hbm, g_hbm, parents_hbm, leaves_hbm, len_hbm,
    gq_out, gks_out, gvs_out, gkp_out, gvp_out,
    q, g, ks, vs, kp, vp, w_s, gp_s, p_half, ds_half, bias, stats, own, sbuf, rbuf,
    gq_ref, gks_ref, gvs_ref, gkp_ref, gvp_ref, parents_ref, leaves_ref, len_ref,
    in_sem, g_send, g_recv, r_send, r_recv, out_sem,
):
    rows, width = q.shape
    heads = width // HD
    kv = ks.shape[1] // HD
    group = heads // kv
    nb = rows // SUF
    local = kp_hbm.shape[0]
    slots = n * local
    chunk = min(slots, 256)
    chunks = slots // chunk
    part = group * HD
    me = lax.axis_index("dp")
    hops = list(range(1, n))
    peers = {j: lax.rem(me + j, n) for j in hops}
    hcol = lambda h: slice(h * HD, (h + 1) * HD)
    brow = lambda b: slice(b * SUF, (b + 1) * SUF)

    def remote(src, dst, send, recv, device):
        return pltpu.make_async_remote_copy(
            src_ref=src, dst_ref=dst, send_sem=send, recv_sem=recv,
            device_id={"dp": device}, device_id_type=MESH,
        )

    barrier = pltpu.get_barrier_semaphore()
    for peer in peers.values():
        pl.semaphore_signal(barrier, inc=1, device_id={"dp": peer}, device_id_type=MESH)

    places = lambda d: pl.ds(pl.multiple_of(d * local, local), local)
    mine = places(me)
    small = [
        pltpu.make_async_copy(parents_hbm, parents_ref, in_sem.at[0]),
        pltpu.make_async_copy(leaves_hbm, leaves_ref, in_sem.at[1]),
        pltpu.make_async_copy(len_hbm, len_ref, in_sem.at[2]),
    ]
    loads = [
        pltpu.make_async_copy(ks_hbm, ks, in_sem.at[3]),
        pltpu.make_async_copy(vs_hbm, vs, in_sem.at[4]),
    ]
    for m in range(kv):
        cols = pl.ds(m * part, part)
        base = 5 + 4 * m
        loads.append(pltpu.make_async_copy(q_hbm.at[:, cols], q.at[:, cols], in_sem.at[base]))
        loads.append(pltpu.make_async_copy(g_hbm.at[:, cols], g.at[:, cols], in_sem.at[base + 1]))
    own_copies = []
    for m in range(kv):
        for w, (src, dst) in enumerate(((kp_hbm, kp), (vp_hbm, vp))):
            own_copies.append(
                pltpu.make_async_copy(src.at[:, hcol(m)], dst.at[m, mine], in_sem.at[7 + 4 * m + w])
            )
    for copy in small + loads + own_copies:
        copy.start()

    sent = []

    def start(copy):
        copy.start()
        sent.append(copy)

    pl.semaphore_wait(barrier, len(hops))
    for m in range(kv):
        for w, (src, dst) in enumerate(((kp_hbm, kp), (vp_hbm, vp))):
            for j in hops:
                start(remote(
                    src.at[:, hcol(m)], dst.at[m, mine], g_send.at[m, w, j], g_recv.at[m, w, me],
                    peers[j],
                ))

    def block_of(m, w, owner):
        held = (kp, vp)[w].at[m, places(owner)]
        return remote(held, held, g_send.at[m, w, 0], g_recv.at[m, w, owner], owner)

    def wait_blocks(m):
        for w in range(2):
            for j in hops:
                block_of(m, w, peers[j]).wait_recv()

    for copy in small:
        copy.wait()
    nodes = len_ref.shape[0]
    place = lax.broadcasted_iota(jnp.int32, (BLK, SUF), 0)
    for b in range(nb):
        current = leaves_ref[b]
        for node in reversed(range(nodes)):
            hit = current == node
            live = jnp.where(hit, len_ref[node], 0)
            current = jnp.where(hit, parents_ref[node], current)
            bias[node * BLK:(node + 1) * BLK, b * SUF:(b + 1) * SUF] = jnp.where(
                place < live, 0.0, LOW
            )

    causal = lax.broadcasted_iota(jnp.int32, (SUF, SUF), 0) <= lax.broadcasted_iota(
        jnp.int32, (SUF, SUF), 1
    )

    loads[0].wait()
    loads[1].wait()
    for h in range(heads):
        m = h // group
        if h % group == 0:
            loads[2 + 2 * m].wait()
            loads[3 + 2 * m].wait()
        for b in range(nb):
            s = dot_nt(ks[brow(b), hcol(m)], q[brow(b), hcol(h)])
            s = jnp.where(causal, s, LOW)
            gp = dot_nt(vs[brow(b), hcol(m)], g[brow(b), hcol(h)])
            top = jnp.max(s, axis=0, keepdims=True)
            w = jnp.exp2((s - top) * EXP_SCALE)
            w_s[h, :, brow(b)] = w
            gp_s[h, :, brow(b)] = gp
            stats[h, 0:1, brow(b)] = top
            stats[h, 1:2, brow(b)] = jnp.sum(w, axis=0, keepdims=True)
            stats[h, 2:3, brow(b)] = jnp.sum(w * gp, axis=0, keepdims=True)

    def partial_to(m, j):
        return remote(
            sbuf.at[m, peers[j]], rbuf.at[m, me], r_send.at[m, j], r_recv.at[m, me], peers[j]
        )

    def partial_from(m, owner):
        return remote(sbuf.at[m, 0], rbuf.at[m, owner], r_send.at[m, 0], r_recv.at[m, owner], owner)

    for copy in own_copies:
        copy.wait()
    for m in range(kv):
        wait_blocks(m)
        for i in range(group):
            h = m * group + i

            def at(c):
                if chunks == 1:
                    return slice(0, chunk)
                return pl.ds(pl.multiple_of(c * chunk, chunk), chunk)

            def scores(c):
                return dot_nt(kp[m, at(c), :], q[:, hcol(h)]) + bias[at(c), :]

            def grads(c):
                return dot_nt(vp[m, at(c), :], g[:, hcol(h)])

            if chunks == 1:
                only_s, only_g = scores(0), grads(0)
                scores, grads = (lambda c: only_s), (lambda c: only_g)
            top_s = stats[h, 0:1, :]
            top = over(
                chunks,
                lambda c, t: jnp.maximum(t, jnp.max(scores(c), axis=0, keepdims=True)),
                top_s,
            )
            shrink = jnp.exp2((top_s - top) * EXP_SCALE)
            weights = lambda c: jnp.exp2((scores(c) - top) * EXP_SCALE)
            if chunks == 1:
                only_w = weights(0)
                weights = lambda c: only_w

            def add_up(c, sums):
                w = weights(c)
                return (
                    sums[0] + jnp.sum(w, axis=0, keepdims=True),
                    sums[1] + jnp.sum(w * grads(c), axis=0, keepdims=True),
                )

            total, dotted = over(
                chunks, add_up, (stats[h, 1:2, :] * shrink, stats[h, 2:3, :] * shrink)
            )
            inverse = 1.0 / total
            delta = dotted * inverse
            stats[h, 3:4, :] = shrink * inverse
            stats[h, 4:5, :] = delta

            def finish(c, nothing):
                probs = weights(c) * inverse
                cols = slice(i * rows, (i + 1) * rows)
                p_half[m, at(c), cols] = probs.astype(jnp.bfloat16)
                ds_half[m, at(c), cols] = (probs * (grads(c) - delta)).astype(jnp.bfloat16)
                return nothing

            over(chunks, finish, 0)

        q_all = jnp.concatenate([q[:, hcol(m * group + i)] for i in range(group)], axis=0)
        g_all = jnp.concatenate([g[:, hcol(m * group + i)] for i in range(group)], axis=0)

        def reduce_node(d, nothing):
            at_d = pl.ds(pl.multiple_of(d * local, local), local)
            put(at_d, d, dot_nn(p_half[m, at_d, :], g_all), dot_nn(ds_half[m, at_d, :], q_all))
            return nothing

        def put(at_d, d, grad_v, grad_k):
            grad_k = grad_k * SCALE
            own[m, 0, at_d, :] = grad_k
            own[m, 1, at_d, :] = grad_v
            sbuf[m, d, 0] = grad_k.astype(jnp.bfloat16)
            sbuf[m, d, 1] = grad_v.astype(jnp.bfloat16)

        if chunks == 1:
            grad_v = dot_nn(p_half[m], g_all)
            grad_k = dot_nn(ds_half[m], q_all)
            for d in range(n):
                at_d = slice(d * local, (d + 1) * local)
                put(at_d, d, grad_v[at_d], grad_k[at_d])
        else:
            lax.fori_loop(0, n, reduce_node, 0)
        for j in hops:
            start(partial_to(m, j))

    results = []
    for m in range(kv):
        kp_t = kp[m].T
        ks_t = [ks[brow(b), hcol(m)].T for b in range(nb)]
        p_parts = [[] for b in range(nb)]
        d_parts = [[] for b in range(nb)]
        for i in range(group):
            h = m * group + i
            probs = w_s[h] * stats[h, 3:4, :]
            ds = (probs * (gp_s[h] - stats[h, 4:5, :])).astype(jnp.bfloat16)
            probs = probs.astype(jnp.bfloat16)
            grad_q = dot_nn(kp_t, ds_half[m, :, i * rows:(i + 1) * rows])
            for b in range(nb):
                p_parts[b].append(probs[:, brow(b)])
                d_parts[b].append(ds[:, brow(b)])
                both = grad_q[:, brow(b)] + dot_nn(ks_t[b], ds[:, brow(b)])
                gq_ref[brow(b), hcol(h)] = (both * SCALE).T.astype(jnp.bfloat16)
        for b in range(nb):
            q_all = jnp.concatenate([q[brow(b), hcol(m * group + i)] for i in range(group)], axis=0)
            g_all = jnp.concatenate([g[brow(b), hcol(m * group + i)] for i in range(group)], axis=0)
            grad_v = dot_nn(jnp.concatenate(p_parts[b], axis=1), g_all)
            grad_k = dot_nn(jnp.concatenate(d_parts[b], axis=1), q_all) * SCALE
            gks_ref[brow(b), hcol(m)] = grad_k.astype(jnp.bfloat16)
            gvs_ref[brow(b), hcol(m)] = grad_v.astype(jnp.bfloat16)
        cols = pl.ds(m * part, part)
        results.append(
            pltpu.make_async_copy(gq_ref.at[:, cols], gq_out.at[:, cols], out_sem.at[4 + m])
        )
        results[-1].start()
        if m == kv - 1:
            results.append(pltpu.make_async_copy(gks_ref, gks_out, out_sem.at[2]))
            results.append(pltpu.make_async_copy(gvs_ref, gvs_out, out_sem.at[3]))
            results[-2].start()
            results[-1].start()

    for m in range(kv):
        for j in hops:
            partial_from(m, peers[j]).wait_recv()
        for w, out in ((0, gkp_ref), (1, gvp_ref)):
            summed = own[m, w, mine, :]
            for j in hops:
                summed = summed + rbuf[m, peers[j], w].astype(jnp.float32)
            out[:, hcol(m)] = summed.astype(jnp.bfloat16)
    last = [
        pltpu.make_async_copy(gkp_ref, gkp_out, out_sem.at[0]),
        pltpu.make_async_copy(gvp_ref, gvp_out, out_sem.at[1]),
    ]
    for copy in last:
        copy.start()
    for copy in sent:
        copy.wait_send()
    for copy in results + last:
        copy.wait()


def write_out(*refs):
    sources, outs, held, sems = refs[:5], refs[5:10], refs[10:15], refs[15]
    loads = [pltpu.make_async_copy(a, b, sems.at[0, i]) for i, (a, b) in enumerate(zip(sources, held))]
    stores = [pltpu.make_async_copy(a, b, sems.at[1, i]) for i, (a, b) in enumerate(zip(held, outs))]
    for copy in loads:
        copy.start()
    for load, store in zip(loads, stores):
        load.wait()
        store.start()
    for copy in stores:
        copy.wait()


def body(n, queries, suffix_keys, suffix_values, prefix_keys, prefix_values, grad_out,
         parents, leaves, node_len):
    rows, width = queries.shape
    kv_width = suffix_keys.shape[1]
    heads, kv = width // HD, kv_width // HD
    group = heads // kv
    local = prefix_keys.shape[0]
    slots = n * local
    half, full = jnp.bfloat16, jnp.float32
    hbm = pl.BlockSpec(memory_space=pl.ANY)
    flops = 10 * rows * heads * HD * (slots + SUF)
    results = pl.pallas_call(
        functools.partial(kernel, n),
        out_shape=(
            jax.ShapeDtypeStruct((rows, width), half),
            jax.ShapeDtypeStruct((rows, kv_width), half),
            jax.ShapeDtypeStruct((rows, kv_width), half),
            jax.ShapeDtypeStruct((local, kv_width), half),
            jax.ShapeDtypeStruct((local, kv_width), half),
        ),
        in_specs=[hbm] * 9,
        out_specs=(hbm,) * 5,
        scratch_shapes=[
            pltpu.VMEM((rows, width), half),
            pltpu.VMEM((rows, width), half),
            pltpu.VMEM((rows, kv_width), half),
            pltpu.VMEM((rows, kv_width), half),
            pltpu.VMEM((kv, slots, HD), half),
            pltpu.VMEM((kv, slots, HD), half),
            pltpu.VMEM((heads, SUF, rows), full),
            pltpu.VMEM((heads, SUF, rows), full),
            pltpu.VMEM((kv, slots, group * rows), half),
            pltpu.VMEM((kv, slots, group * rows), half),
            pltpu.VMEM((slots, rows), full),
            pltpu.VMEM((heads, 8, rows), full),
            pltpu.VMEM((kv, 2, slots, HD), full),
            pltpu.VMEM((kv, n, 2, local, HD), half),
            pltpu.VMEM((kv, n, 2, local, HD), half),
            pltpu.VMEM((rows, width), half),
            pltpu.VMEM((rows, kv_width), half),
            pltpu.VMEM((rows, kv_width), half),
            pltpu.VMEM((local, kv_width), half),
            pltpu.VMEM((local, kv_width), half),
            pltpu.SMEM(parents.shape, jnp.int32),
            pltpu.SMEM(leaves.shape, jnp.int32),
            pltpu.SMEM(node_len.shape, jnp.int32),
            pltpu.SemaphoreType.DMA((5 + 4 * kv,)),
            pltpu.SemaphoreType.DMA((kv, 2, n)),
            pltpu.SemaphoreType.DMA((kv, 2, n)),
            pltpu.SemaphoreType.DMA((kv, n)),
            pltpu.SemaphoreType.DMA((kv, n)),
            pltpu.SemaphoreType.DMA((4 + kv,)),
        ],
        compiler_params=pltpu.CompilerParams(
            collective_id=0, has_side_effects=True, vmem_limit_bytes=LIMIT
        ),
        cost_estimate=pl.CostEstimate(
            flops=flops, bytes_accessed=8 * rows * width, transcendentals=rows * heads * (slots + SUF)
        ),
    )(queries, suffix_keys, suffix_values, prefix_keys, prefix_values, grad_out,
      parents, leaves, node_len)
    return pl.pallas_call(
        write_out,
        out_shape=tuple(jax.ShapeDtypeStruct(r.shape, r.dtype) for r in results),
        in_specs=[pl.BlockSpec(memory_space=pl.ANY)] * 5,
        out_specs=(hbm,) * 5,
        scratch_shapes=[pltpu.VMEM(r.shape, r.dtype) for r in results]
        + [pltpu.SemaphoreType.DMA((2, 5))],
        compiler_params=pltpu.CompilerParams(vmem_limit_bytes=LIMIT),
        cost_estimate=pl.CostEstimate(flops=0, bytes_accessed=4 * rows * width, transcendentals=0),
    )(*results)


def solution(mesh):
    rows_cols = P(("groups", "dp"), "tensor")
    return jax.shard_map(
        functools.partial(body, mesh.shape["dp"]),
        mesh=mesh,
        in_specs=(rows_cols,) * 6 + (P("groups"), P(("groups", "dp")), P("groups")),
        out_specs=(rows_cols,) * 5,
        check_vma=False,
    )
```

```python
import functools
import math

import jax
import jax.numpy as jnp
from jax import lax
from jax.experimental import pallas as pl
from jax.experimental.pallas import tpu as pltpu
from jax.sharding import PartitionSpec as P

HD = 128
BLK = 64
SUF = 128
SCALE = HD ** -0.5
EXP_SCALE = SCALE * math.log2(math.e)
LOW = -1e30
LIMIT = 63 * 1024 * 1024
MESH = pl.DeviceIdType.MESH


def dot_nt(left, right):
    return lax.dot_general(
        left, right, (((1,), (1,)), ((), ())), preferred_element_type=jnp.float32
    )


def dot_nn(left, right):
    return jnp.dot(left, right, preferred_element_type=jnp.float32)


def over(count, step, start):
    if count == 1:
        return step(0, start)
    return lax.fori_loop(0, count, step, start)


def kernel(
    n,
    q_hbm, ks_hbm, vs_hbm, kp_hbm, vp_hbm, g_hbm, parents_hbm, leaves_hbm, len_hbm,
    gq_out, gks_out, gvs_out, gkp_out, gvp_out,
    q, g, ks, vs, kp, vp, w_s, gp_s, p_half, ds_half, bias, stats, own, sbuf, rbuf,
    gq_ref, gks_ref, gvs_ref, gkp_ref, gvp_ref, parents_ref, leaves_ref, len_ref,
    in_sem, g_send, g_recv, r_send, r_recv, out_sem,
):
    rows, width = q.shape
    heads = width // HD
    kv = ks.shape[1] // HD
    group = heads // kv
    nb = rows // SUF
    local = kp_hbm.shape[0]
    slots = n * local
    chunk = min(slots, 256)
    chunks = slots // chunk
    part = group * HD
    me = lax.axis_index("dp")
    hops = list(range(1, n))
    low = me < n // 2
    rising = {j: jnp.where(j <= me, j - 1, j) for j in hops}
    falling = {j: jnp.where(n - j > me, n - j, n - 1 - j) for j in hops}
    peers = {j: jnp.where(low, falling[j], rising[j]) for j in hops}
    hcol = lambda h: slice(h * HD, (h + 1) * HD)
    brow = lambda b: slice(b * SUF, (b + 1) * SUF)

    def remote(src, dst, send, recv, device):
        return pltpu.make_async_remote_copy(
            src_ref=src, dst_ref=dst, send_sem=send, recv_sem=recv,
            device_id={"dp": device}, device_id_type=MESH,
        )

    barrier = pltpu.get_barrier_semaphore()
    for peer in peers.values():
        pl.semaphore_signal(barrier, inc=1, device_id={"dp": peer}, device_id_type=MESH)

    places = lambda d: pl.ds(pl.multiple_of(d * local, local), local)
    mine = places(me)
    small = [
        pltpu.make_async_copy(parents_hbm, parents_ref, in_sem.at[0]),
        pltpu.make_async_copy(leaves_hbm, leaves_ref, in_sem.at[1]),
        pltpu.make_async_copy(len_hbm, len_ref, in_sem.at[2]),
    ]
    loads = [
        pltpu.make_async_copy(ks_hbm, ks, in_sem.at[3]),
        pltpu.make_async_copy(vs_hbm, vs, in_sem.at[4]),
    ]
    for m in range(kv):
        cols = pl.ds(m * part, part)
        base = 5 + 4 * m
        loads.append(pltpu.make_async_copy(q_hbm.at[:, cols], q.at[:, cols], in_sem.at[base]))
        loads.append(pltpu.make_async_copy(g_hbm.at[:, cols], g.at[:, cols], in_sem.at[base + 1]))
    own_copies = []
    for m in range(kv):
        for w, (src, dst) in enumerate(((kp_hbm, kp), (vp_hbm, vp))):
            own_copies.append(
                pltpu.make_async_copy(src.at[:, hcol(m)], dst.at[m, mine], in_sem.at[7 + 4 * m + w])
            )
    for copy in small + loads + own_copies:
        copy.start()

    sent = []

    def start(copy):
        copy.start()
        sent.append(copy)

    pl.semaphore_wait(barrier, len(hops))
    for m in range(kv):
        for w, (src, dst) in enumerate(((kp_hbm, kp), (vp_hbm, vp))):
            for j in hops:
                start(remote(
                    src.at[:, hcol(m)], dst.at[m, mine], g_send.at[m, w, j], g_recv.at[m, w, me],
                    peers[j],
                ))

    def block_of(m, w, owner):
        held = (kp, vp)[w].at[m, places(owner)]
        return remote(held, held, g_send.at[m, w, 0], g_recv.at[m, w, owner], owner)

    def wait_blocks(m):
        for w in range(2):
            for j in hops:
                block_of(m, w, peers[j]).wait_recv()

    for copy in small:
        copy.wait()
    nodes = len_ref.shape[0]
    place = lax.broadcasted_iota(jnp.int32, (BLK, SUF), 0)
    for b in range(nb):
        current = leaves_ref[b]
        for node in reversed(range(nodes)):
            hit = current == node
            live = jnp.where(hit, len_ref[node], 0)
            current = jnp.where(hit, parents_ref[node], current)
            bias[node * BLK:(node + 1) * BLK, b * SUF:(b + 1) * SUF] = jnp.where(
                place < live, 0.0, LOW
            )

    causal = lax.broadcasted_iota(jnp.int32, (SUF, SUF), 0) <= lax.broadcasted_iota(
        jnp.int32, (SUF, SUF), 1
    )

    loads[0].wait()
    loads[1].wait()
    for h in range(heads):
        m = h // group
        if h % group == 0:
            loads[2 + 2 * m].wait()
            loads[3 + 2 * m].wait()
        for b in range(nb):
            s = dot_nt(ks[brow(b), hcol(m)], q[brow(b), hcol(h)])
            s = jnp.where(causal, s, LOW)
            gp = dot_nt(vs[brow(b), hcol(m)], g[brow(b), hcol(h)])
            top = jnp.max(s, axis=0, keepdims=True)
            w = jnp.exp2((s - top) * EXP_SCALE)
            w_s[h, :, brow(b)] = w
            gp_s[h, :, brow(b)] = gp
            stats[h, 0:1, brow(b)] = top
            stats[h, 1:2, brow(b)] = jnp.sum(w, axis=0, keepdims=True)
            stats[h, 2:3, brow(b)] = jnp.sum(w * gp, axis=0, keepdims=True)

    def partial_to(m, j):
        return remote(
            sbuf.at[m, peers[j]], rbuf.at[m, me], r_send.at[m, j], r_recv.at[m, me], peers[j]
        )

    def partial_from(m, owner):
        return remote(sbuf.at[m, 0], rbuf.at[m, owner], r_send.at[m, 0], r_recv.at[m, owner], owner)

    for copy in own_copies:
        copy.wait()
    for m in range(kv):
        wait_blocks(m)
        for i in range(group):
            h = m * group + i

            def at(c):
                if chunks == 1:
                    return slice(0, chunk)
                return pl.ds(pl.multiple_of(c * chunk, chunk), chunk)

            def scores(c):
                return dot_nt(kp[m, at(c), :], q[:, hcol(h)]) + bias[at(c), :]

            def grads(c):
                return dot_nt(vp[m, at(c), :], g[:, hcol(h)])

            if chunks == 1:
                only_s, only_g = scores(0), grads(0)
                scores, grads = (lambda c: only_s), (lambda c: only_g)
            top_s = stats[h, 0:1, :]
            top = over(
                chunks,
                lambda c, t: jnp.maximum(t, jnp.max(scores(c), axis=0, keepdims=True)),
                top_s,
            )
            shrink = jnp.exp2((top_s - top) * EXP_SCALE)
            weights = lambda c: jnp.exp2((scores(c) - top) * EXP_SCALE)
            if chunks == 1:
                only_w = weights(0)
                weights = lambda c: only_w

            def add_up(c, sums):
                w = weights(c)
                return (
                    sums[0] + jnp.sum(w, axis=0, keepdims=True),
                    sums[1] + jnp.sum(w * grads(c), axis=0, keepdims=True),
                )

            total, dotted = over(
                chunks, add_up, (stats[h, 1:2, :] * shrink, stats[h, 2:3, :] * shrink)
            )
            inverse = 1.0 / total
            delta = dotted * inverse
            stats[h, 3:4, :] = shrink * inverse
            stats[h, 4:5, :] = delta

            def finish(c, nothing):
                probs = weights(c) * inverse
                cols = slice(i * rows, (i + 1) * rows)
                p_half[m, at(c), cols] = probs.astype(jnp.bfloat16)
                ds_half[m, at(c), cols] = (probs * (grads(c) - delta)).astype(jnp.bfloat16)
                return nothing

            over(chunks, finish, 0)

        q_all = jnp.concatenate([q[:, hcol(m * group + i)] for i in range(group)], axis=0)
        g_all = jnp.concatenate([g[:, hcol(m * group + i)] for i in range(group)], axis=0)

        def reduce_node(d, nothing):
            at_d = pl.ds(pl.multiple_of(d * local, local), local)
            put(at_d, d, dot_nn(p_half[m, at_d, :], g_all), dot_nn(ds_half[m, at_d, :], q_all))
            return nothing

        def put(at_d, d, grad_v, grad_k):
            grad_k = grad_k * SCALE
            own[m, 0, at_d, :] = grad_k
            own[m, 1, at_d, :] = grad_v
            sbuf[m, d, 0] = grad_k.astype(jnp.bfloat16)
            sbuf[m, d, 1] = grad_v.astype(jnp.bfloat16)

        if chunks == 1:
            grad_v = dot_nn(p_half[m], g_all)
            grad_k = dot_nn(ds_half[m], q_all)
            for d in range(n):
                at_d = slice(d * local, (d + 1) * local)
                put(at_d, d, grad_v[at_d], grad_k[at_d])
        else:
            lax.fori_loop(0, n, reduce_node, 0)
        for j in hops:
            start(partial_to(m, j))

    results = []
    for m in range(kv):
        kp_t = kp[m].T
        ks_t = [ks[brow(b), hcol(m)].T for b in range(nb)]
        p_parts = [[] for b in range(nb)]
        d_parts = [[] for b in range(nb)]
        for i in range(group):
            h = m * group + i
            probs = w_s[h] * stats[h, 3:4, :]
            ds = (probs * (gp_s[h] - stats[h, 4:5, :])).astype(jnp.bfloat16)
            probs = probs.astype(jnp.bfloat16)
            grad_q = dot_nn(kp_t, ds_half[m, :, i * rows:(i + 1) * rows])
            for b in range(nb):
                p_parts[b].append(probs[:, brow(b)])
                d_parts[b].append(ds[:, brow(b)])
                both = grad_q[:, brow(b)] + dot_nn(ks_t[b], ds[:, brow(b)])
                gq_ref[brow(b), hcol(h)] = (both * SCALE).T.astype(jnp.bfloat16)
        for b in range(nb):
            q_all = jnp.concatenate([q[brow(b), hcol(m * group + i)] for i in range(group)], axis=0)
            g_all = jnp.concatenate([g[brow(b), hcol(m * group + i)] for i in range(group)], axis=0)
            grad_v = dot_nn(jnp.concatenate(p_parts[b], axis=1), g_all)
            grad_k = dot_nn(jnp.concatenate(d_parts[b], axis=1), q_all) * SCALE
            gks_ref[brow(b), hcol(m)] = grad_k.astype(jnp.bfloat16)
            gvs_ref[brow(b), hcol(m)] = grad_v.astype(jnp.bfloat16)
        cols = pl.ds(m * part, part)
        results.append(
            pltpu.make_async_copy(gq_ref.at[:, cols], gq_out.at[:, cols], out_sem.at[4 + m])
        )
        results[-1].start()
        if m == kv - 1:
            results.append(pltpu.make_async_copy(gks_ref, gks_out, out_sem.at[2]))
            results.append(pltpu.make_async_copy(gvs_ref, gvs_out, out_sem.at[3]))
            results[-2].start()
            results[-1].start()

    for m in range(kv):
        for j in hops:
            partial_from(m, peers[j]).wait_recv()
        for w, out in ((0, gkp_ref), (1, gvp_ref)):
            summed = own[m, w, mine, :]
            for j in hops:
                summed = summed + rbuf[m, peers[j], w].astype(jnp.float32)
            out[:, hcol(m)] = summed.astype(jnp.bfloat16)
    last = [
        pltpu.make_async_copy(gkp_ref, gkp_out, out_sem.at[0]),
        pltpu.make_async_copy(gvp_ref, gvp_out, out_sem.at[1]),
    ]
    for copy in last:
        copy.start()
    for copy in sent:
        copy.wait_send()
    for copy in results + last:
        copy.wait()


def write_out(*refs):
    sources, outs, held, sems = refs[:5], refs[5:10], refs[10:15], refs[15]
    loads = [pltpu.make_async_copy(a, b, sems.at[0, i]) for i, (a, b) in enumerate(zip(sources, held))]
    stores = [pltpu.make_async_copy(a, b, sems.at[1, i]) for i, (a, b) in enumerate(zip(held, outs))]
    for copy in loads:
        copy.start()
    for load, store in zip(loads, stores):
        load.wait()
        store.start()
    for copy in stores:
        copy.wait()


def body(n, queries, suffix_keys, suffix_values, prefix_keys, prefix_values, grad_out,
         parents, leaves, node_len):
    rows, width = queries.shape
    kv_width = suffix_keys.shape[1]
    heads, kv = width // HD, kv_width // HD
    group = heads // kv
    local = prefix_keys.shape[0]
    slots = n * local
    half, full = jnp.bfloat16, jnp.float32
    hbm = pl.BlockSpec(memory_space=pl.ANY)
    flops = 10 * rows * heads * HD * (slots + SUF)
    results = pl.pallas_call(
        functools.partial(kernel, n),
        out_shape=(
            jax.ShapeDtypeStruct((rows, width), half),
            jax.ShapeDtypeStruct((rows, kv_width), half),
            jax.ShapeDtypeStruct((rows, kv_width), half),
            jax.ShapeDtypeStruct((local, kv_width), half),
            jax.ShapeDtypeStruct((local, kv_width), half),
        ),
        in_specs=[hbm] * 9,
        out_specs=(hbm,) * 5,
        scratch_shapes=[
            pltpu.VMEM((rows, width), half),
            pltpu.VMEM((rows, width), half),
            pltpu.VMEM((rows, kv_width), half),
            pltpu.VMEM((rows, kv_width), half),
            pltpu.VMEM((kv, slots, HD), half),
            pltpu.VMEM((kv, slots, HD), half),
            pltpu.VMEM((heads, SUF, rows), full),
            pltpu.VMEM((heads, SUF, rows), full),
            pltpu.VMEM((kv, slots, group * rows), half),
            pltpu.VMEM((kv, slots, group * rows), half),
            pltpu.VMEM((slots, rows), full),
            pltpu.VMEM((heads, 8, rows), full),
            pltpu.VMEM((kv, 2, slots, HD), full),
            pltpu.VMEM((kv, n, 2, local, HD), half),
            pltpu.VMEM((kv, n, 2, local, HD), half),
            pltpu.VMEM((rows, width), half),
            pltpu.VMEM((rows, kv_width), half),
            pltpu.VMEM((rows, kv_width), half),
            pltpu.VMEM((local, kv_width), half),
            pltpu.VMEM((local, kv_width), half),
            pltpu.SMEM(parents.shape, jnp.int32),
            pltpu.SMEM(leaves.shape, jnp.int32),
            pltpu.SMEM(node_len.shape, jnp.int32),
            pltpu.SemaphoreType.DMA((5 + 4 * kv,)),
            pltpu.SemaphoreType.DMA((kv, 2, n)),
            pltpu.SemaphoreType.DMA((kv, 2, n)),
            pltpu.SemaphoreType.DMA((kv, n)),
            pltpu.SemaphoreType.DMA((kv, n)),
            pltpu.SemaphoreType.DMA((4 + kv,)),
        ],
        compiler_params=pltpu.CompilerParams(
            collective_id=0, has_side_effects=True, vmem_limit_bytes=LIMIT
        ),
        cost_estimate=pl.CostEstimate(
            flops=flops, bytes_accessed=8 * rows * width, transcendentals=rows * heads * (slots + SUF)
        ),
    )(queries, suffix_keys, suffix_values, prefix_keys, prefix_values, grad_out,
      parents, leaves, node_len)
    return pl.pallas_call(
        write_out,
        out_shape=tuple(jax.ShapeDtypeStruct(r.shape, r.dtype) for r in results),
        in_specs=[pl.BlockSpec(memory_space=pl.ANY)] * 5,
        out_specs=(hbm,) * 5,
        scratch_shapes=[pltpu.VMEM(r.shape, r.dtype) for r in results]
        + [pltpu.SemaphoreType.DMA((2, 5))],
        compiler_params=pltpu.CompilerParams(vmem_limit_bytes=LIMIT),
        cost_estimate=pl.CostEstimate(flops=0, bytes_accessed=4 * rows * width, transcendentals=0),
    )(*results)


def solution(mesh):
    rows_cols = P(("groups", "dp"), "tensor")
    return jax.shard_map(
        functools.partial(body, mesh.shape["dp"]),
        mesh=mesh,
        in_specs=(rows_cols,) * 6 + (P("groups"), P(("groups", "dp")), P("groups")),
        out_specs=(rows_cols,) * 5,
        check_vma=False,
    )
```
